128 devices in a mesh: tok: 4 (over x), voc: 8 (over z, core), section: 4 (over y).
Axes of the slice: x: 4, y: 4, z: 4, core: 2. Of those that a mesh axis runs over, the one named last changes fastest.
Arguments:
- hidden: bfloat16 [512, 4608], P('tok'), may hold values from -8 to 8
- head_weight: bfloat16 [128000, 4608], P(('tok', 'voc', 'section')), may hold values from -1 to 1
- teacher_logits: bfloat16 [512, 128000], P(('voc', 'section'), 'tok'), may hold values from -400 to 400
- token_weight: float32 [512], replicated, may hold values from 4 to 40
- token_ids: int32 [512], replicated, may hold values from 0 to 127999
- embed_grad: bfloat16 [512, 4608], P('tok'), may hold values from -6 to 6
Outputs:
- grad_hidden: bfloat16 [512, 4608], P('tok')
- grad_head: bfloat16 [128000, 4608], P(('tok', 'voc', 'section'))
The draws below stay inside these ranges and needn't reach their ends.
All inputs are finite; a program needn't handle non-finite values.
Results may differ from the reference program's by a relative error of at most 0.0051.
Values may be sent and summed in bfloat16 or wider, within the bound.
A program may use at most 192 MiB of HBM per device.

```python
import math
import jax
import jax.numpy as jnp
import numpy as np

D = 4608
V = 128000
TOKENS = 512


def draw_hidden(key, part):
    key = jax.random.fold_in(key, 11)
    values = jnp.clip(jax.random.normal(key, (TOKENS, D), jnp.float32), -6.0, 6.0)
    return values.astype(jnp.bfloat16)


def draw_head_weight(key, part):
    key = jax.random.fold_in(key, 23)
    spread = 3.0 / D ** 0.5
    values = spread * jnp.clip(jax.random.normal(key, (V, D), jnp.float32), -6.0, 6.0)
    return values.astype(jnp.bfloat16)


def draw_teacher_logits(key, part):
    key = jax.random.fold_in(key, 37)
    values = 3.0 * jnp.clip(jax.random.normal(key, (TOKENS, V), jnp.float32), -6.0, 6.0)
    return values.astype(jnp.bfloat16)


def place_ends(array, rng, low, largest):
    longest = array.shape.index(max(array.shape))
    spots = []
    for shift in (0, 1):
        where = [jax.random.randint(jax.random.fold_in(rng, axis), (), 0, length) for axis, length in enumerate(array.shape)]
        where[longest] = (where[longest] + shift) % array.shape[longest]
        spots.append(tuple(where))
    return array.at[spots[0]].set(low).at[spots[1]].set(largest)


def levels(own_key, shape, shards, low, largest):
    level = 1.0
    for axis_at, shards_of in shards:
        steps = jax.random.uniform(jax.random.fold_in(jax.random.fold_in(own_key, 6), axis_at), (shards_of,), jnp.float32, low / len(shards), largest / len(shards))
        level = level * jnp.repeat(jnp.exp(steps), shape[axis_at] // shards_of).reshape((-1,) + (1,) * (len(shape) - 1 - axis_at))
    return level


def wide_ids(rng, shape, number_of, lean):
    portions = [min(1 << octave, number_of + 1 - (1 << octave)) * (1 << 20) // math.isqrt((1 << octave) ** lean) + 1 for octave in range((number_of + 1).bit_length()) if 1 << octave <= number_of]
    deviation = 1 + sum(portions) // (1 << 30)
    grid = np.cumsum(np.array([max(1, weight // deviation) for weight in portions]))
    ticket = jax.random.randint(jax.random.fold_in(rng, 1), shape, 0, int(grid[len(portions) - 1]))
    start = jnp.left_shift(1, jnp.searchsorted(jnp.asarray(grid, jnp.int32), ticket, side="right").astype(jnp.int32))
    grade = start - 1 + jax.random.randint(jax.random.fold_in(rng, 4), shape, 0, 1 << 30) % jnp.minimum(start, number_of + 1 - start)
    return jax.random.permutation(jax.random.fold_in(rng, 2), number_of)[grade].astype(jnp.int32)


def centred(stream_key, shape, scale, most, cuts=(), held_as=jnp.bfloat16):
    entries = scale * jax.random.normal(stream_key, shape, jnp.float32)
    if cuts:
        entries = entries * levels(stream_key, shape, cuts, -0.22, 0.18)
    return jnp.clip(entries, -most, most).astype(held_as)


def setup_inputs(seed: int = 0) -> dict:
    streams_of = jax.random.split(jax.random.key(seed), 7)
    return {
        "hidden": draw_hidden(jax.random.fold_in(streams_of[6], 71), 0),
        "head_weight": draw_head_weight(jax.random.fold_in(streams_of[6], 71), 0),
        "teacher_logits": draw_teacher_logits(jax.random.fold_in(streams_of[6], 71), 0),
        "token_weight": jnp.clip(jnp.exp(jax.random.uniform(streams_of[3], (TOKENS,), jnp.float32, math.log(4.0), math.log(40.0))), 4.0, 40.0),
        "token_ids": place_ends(wide_ids(streams_of[4], (TOKENS,), V, 2), jax.random.fold_in(streams_of[4], 3), 0, V - 1).astype(jnp.int32),
        "embed_grad": centred(streams_of[5], (TOKENS, D), 1.0, 6.0, ((0, 4),)),
    }


def softmax_rows(values):
    top = jnp.max(values, axis=1, keepdims=True)
    terms = jnp.exp(values - top)
    return terms / jnp.sum(terms, axis=1, keepdims=True)


def reference(hidden, head_weight, teacher_logits, token_weight, token_ids, embed_grad):
    student = jnp.dot(hidden, head_weight.T, preferred_element_type=jnp.float32)
    student_prob = softmax_rows(student)
    teacher_prob = softmax_rows(teacher_logits.astype(jnp.float32))
    dlogits = (token_weight[:, None] * (student_prob - teacher_prob)).astype(jnp.bfloat16)
    grad_hidden = jnp.dot(dlogits, head_weight, preferred_element_type=jnp.float32).astype(jnp.bfloat16)
    head_part = jnp.dot(dlogits.T, hidden, preferred_element_type=jnp.float32)
    head_part = head_part.at[token_ids.astype(jnp.int32)].add(embed_grad.astype(jnp.float32))
    return grad_hidden, head_part.astype(jnp.bfloat16)
```

```python
import functools

import jax
import jax.numpy as jnp
from jax import lax
from jax.experimental import pallas as pl
from jax.experimental.pallas import tpu as pltpu
from jax.sharding import PartitionSpec as P

MESH = pl.DeviceIdType.MESH
D = 4608
ROWS = 1000
WIDE = 1152
COLS = 32000
C = 768
HC = 384
LOW = -1e30
F32 = jnp.float32
BF16 = jnp.bfloat16


def merge(tiles):
    top = functools.reduce(jnp.maximum, [t[0:4] for t in tiles])
    total = sum(t[4:8] * jnp.exp(t[0:4] - top) for t in tiles)
    return top, total


def kernel(hidden, weight, teacher, tw, ids, embed, gh_out, head_out,
           he, w, tl, tr, tT, sT, lhs, dl, st, tt, sr, trr,
           cs, cr, s1, r10, r11, r12, s20, s21, s22, r20, r21, r22,
           s30, s31, s32, r3, go, gb, ssem, rsem, lsem, stop=99):
    x = lax.axis_index("tok")
    v = lax.axis_index("voc")
    y = lax.axis_index("section")
    z, c = v // 2, v % 2
    j = v * 4 + y
    zh, zl = z // 2, z % 2
    zcols = pl.ds(pl.multiple_of(zl * HC, 128), HC)

    def xp(d):
        return ((x + d) % 4, v, y)

    def yp(d):
        return (x, v, (y + d) % 4)

    def zp(d):
        return (x, (v + 2 * d) % 8, y)

    def vp(d):
        return (x, (v + d) % 8, y)

    def pp(d):
        other = (j + d) % 32
        return (x, other // 4, other % 4)

    sibling = (x, v + 1 - 2 * c, y)
    count = [0]
    sent = []

    def send(src, dst, to):
        i = count[0]
        count[0] += 1
        copy = pltpu.make_async_remote_copy(
            src, dst, ssem.at[i], rsem.at[i], device_id=to, device_id_type=MESH)
        copy.start()
        sent.append(copy)
        return copy

    lcount = [0]

    def local(src, dst):
        i = lcount[0]
        lcount[0] += 1
        copy = pltpu.make_async_copy(src, dst, lsem.at[i])
        copy.start()
        return copy

    def arrive(copies):
        for copy in copies:
            copy.wait_recv()

    own_hidden = [local(hidden.at[:, :, :, pl.ds(k * C, C)], he.at[k, 0]) for k in range(6)]
    own_teacher = local(teacher, tl)
    own_weight = local(weight, w)
    own_embed = [local(embed.at[:, :, :, pl.ds(k * C, C)], he.at[k, 4]) for k in range(6)]

    barrier = pltpu.get_barrier_semaphore()
    for d in range(1, 4):
        pl.semaphore_signal(barrier, inc=1, device_id=xp(d), device_id_type=MESH)
    for d in range(1, 32):
        pl.semaphore_signal(barrier, inc=1, device_id=pp(d), device_id_type=MESH)
    pl.semaphore_wait(barrier, 34)

    for copy in own_hidden:
        copy.wait()
    k0, k1, k2 = c * 3, c * 3 + 1, c * 3 + 2
    order = (1, 3, 2)
    hx = {}
    for k, p in ((k1, 1), (k2, 2)):
        hx[p] = [send(he.at[k, 0, y, zh, :, zcols], he.at[k, 4 - d, y, zh, :, zcols], xp(d)) for d in order]
    hx[0] = [send(he.at[k0, 0], he.at[k0, 4 - d], xp(d)) for d in order]
    arrive(hx[1])
    part = he.at[k1, pl.ds(1, 3), y, zh, :, zcols]
    hy1 = [send(part, part, yp(d)) for d in order]
    arrive(hx[2])
    part = he.at[k2, pl.ds(1, 3), y, zh, :, zcols]
    hz2 = [send(part, part, zp(d)) for d in order]
    arrive(hy1)
    part = he.at[k1, pl.ds(1, 3), :, zh, :, zcols]
    hz1 = [send(part, part, zp(d)) for d in order]
    arrive(hz2)
    part = he.at[k2, pl.ds(1, 3), y]
    hy2 = [send(part, part, yp(d)) for d in order]

    def start_of(device):
        return pl.multiple_of(jnp.minimum(device * ROWS // 128 * 128, COLS - WIDE), 128)

    own_teacher.wait()
    teach = []
    for d in range(1, 32):
        teach.append(send(tl.at[:, pl.ds(start_of((j + d) % 32), WIDE)], tr.at[j], pp(d)))
    own_block = local(tl.at[:, pl.ds(start_of(j), WIDE)], tr.at[j])

    def max_step(i, acc):
        for q in range(10):
            acc = jnp.maximum(acc, tl[:, pl.ds(pl.multiple_of((i * 10 + q) * 128, 128), 128)].astype(F32))
        return acc

    ttop = jnp.max(lax.fori_loop(0, COLS // 1280, max_step, jnp.full((16, 128), LOW, F32)), axis=1, keepdims=True)

    def sum_step(i, acc):
        for q in range(10):
            acc = acc + jnp.exp(tl[:, pl.ds(pl.multiple_of((i * 10 + q) * 128, 128), 128)].astype(F32) - ttop)
        return acc

    ttot = jnp.sum(lax.fori_loop(0, COLS // 1280, sum_step, jnp.zeros((16, 128), F32)), axis=1, keepdims=True)
    lane = lax.broadcasted_iota(jnp.int32, (16, 128), 1)
    row = lax.broadcasted_iota(jnp.int32, (16, 128), 0)
    here = lane == row + (j % 8) * 16
    tt[0, 0:4] = jnp.full((4, 128), LOW, F32)
    tt[0, 4:8] = jnp.zeros((4, 128), F32)
    tt[0, pl.ds(j // 8, 1)] = jnp.max(jnp.where(here, jnp.broadcast_to(ttop, (16, 128)), LOW), axis=0, keepdims=True)
    tt[0, pl.ds(4 + j // 8, 1)] = jnp.sum(jnp.where(here, jnp.broadcast_to(ttot, (16, 128)), 0.0), axis=0, keepdims=True)

    def stage(buf, rec, n, base, peers):
        return [send(buf.at[n], rec.at[base + i], peer) for i, peer in enumerate(peers)]

    def join(buf, rec, n, base, copies):
        arrive(copies)
        top, total = merge([buf[n]] + [rec[base + i] for i in range(len(copies))])
        buf[n + 1, 0:4] = top
        buf[n + 1, 4:8] = total

    vpeers = [vp(d) for d in range(1, 8)]
    ypeers = [yp(d) for d in order]
    xpeers = [xp(d) for d in order]
    ts = stage(tt, trr, 0, 0, vpeers)

    def student(k, first):
        for half in range(2):
            tok = he[k, 2 * half:2 * half + 2].reshape(256, C)
            cols = slice(half * 256, half * 256 + 256)
            part = lax.dot_general(w[:, pl.ds(pl.multiple_of(k * C, 128), C)], tok,
                                   (((1,), (1,)), ((), ())), preferred_element_type=F32)
            if first:
                sT[0:ROWS, cols] = part
            else:
                sT[0:ROWS, cols] += part

    arrive(hx[0])
    hc = [send(he.at[k0, pl.ds(1, 3)], he.at[k0, pl.ds(1, 3)], sibling)]
    for copy in own_embed:
        copy.wait()
    ex = []
    for d in order:
        for p in range(3):
            ex.append(send(he.at[c * 3 + p, 4], he.at[c * 3 + p, 8 - d], xp(d)))
    own_weight.wait()
    student(k0, True)
    arrive(hz1)
    hc.append(send(he.at[k1, pl.ds(1, 3)], he.at[k1, pl.ds(1, 3)], sibling))
    arrive(hy2)
    hc.append(send(he.at[k2, pl.ds(1, 3)], he.at[k2, pl.ds(1, 3)], sibling))
    student(k1, False)
    join(tt, trr, 0, 0, ts)
    ts = stage(tt, trr, 1, 7, ypeers)
    student(k2, False)
    for p in range(3):
        arrive([hc[p]])
        student((1 - c) * 3 + p, False)
        if p == 0:
            join(tt, trr, 1, 7, ts)
            ts = stage(tt, trr, 2, 10, xpeers)

    def smax_step(i, acc):
        block = sT[pl.ds(pl.multiple_of(i * 40, 8), 40), :]
        for q in range(5):
            acc = jnp.maximum(acc, block[q * 8:q * 8 + 8])
        return acc

    stop_ = jnp.max(lax.fori_loop(0, 25, smax_step, jnp.full((8, 512), -3e38, F32)), axis=0, keepdims=True)

    def ssum_step(i, acc):
        at = pl.ds(pl.multiple_of(i * 40, 8), 40)
        block = jnp.exp(sT[at, :] - stop_)
        sT[at, :] = block
        for q in range(5):
            acc = acc + block[q * 8:q * 8 + 8]
        return acc

    stot = jnp.sum(lax.fori_loop(0, 25, ssum_step, jnp.zeros((8, 512), F32)), axis=0, keepdims=True)
    blocks = [(x + r) % 4 for r in range(4)]
    for r in range(4):
        st[0, pl.ds(blocks[r], 1)] = stop_[:, r * 128:r * 128 + 128]
        st[0, pl.ds(4 + blocks[r], 1)] = stot[:, r * 128:r * 128 + 128]
    ss = stage(st, sr, 0, 0, vpeers)

    lhs[ROWS - 8:1024, :] = jnp.zeros((1024 - ROWS + 8, 1024), BF16)
    idrow = jnp.concatenate([ids[pl.ds(blocks[r], 1), :] for r in range(4)], axis=1) - (x * COLS + j * ROWS)

    def onehot(i, _):
        at = pl.multiple_of(i * 32, 32)
        rows = lax.broadcasted_iota(jnp.int32, (32, 512), 0) + at
        lhs[pl.ds(at, 32), 512:1024] = jnp.where((rows == idrow) & (rows < ROWS), 1.0, 0.0).astype(BF16)
        return 0

    lax.fori_loop(0, 32, onehot, 0)
    join(st, sr, 0, 0, ss)
    ss = stage(st, sr, 1, 7, ypeers)
    join(tt, trr, 2, 10, ts)
    join(st, sr, 1, 7, ss)
    ss = stage(st, sr, 2, 10, xpeers)
    join(st, sr, 2, 10, ss)

    weights = tw[...]
    st[4, 0:4] = weights / st[3, 4:8]
    tt[4, 0:4] = weights / tt[3, 4:8]

    def token_row(ref, n, base):
        return jnp.concatenate([ref[n, pl.ds(base + blocks[r], 1), :] for r in range(4)], axis=1)

    sfac = jnp.exp(stop_ - token_row(st, 3, 0)) * token_row(st, 4, 0)
    tfac = token_row(tt, 4, 0)
    tmax = token_row(tt, 3, 0)

    own_block.wait()
    arrive(teach)
    tT[:, WIDE:WIDE + 32, :] = jnp.zeros((4, 32, 128), F32)
    for r in range(4):
        at = pl.multiple_of(blocks[r] * 8, 8)
        for q in range(9):
            tile = tr[pl.ds(at, 8), :, q * 128:q * 128 + 128].reshape(128, 128).astype(F32)
            tT[r, q * 128:q * 128 + 128, :] = tile.T

    shift = j * ROWS - start_of(j)

    def dstep(i, _):
        at = pl.multiple_of(i * 128, 128)
        rows = lax.broadcasted_iota(jnp.int32, (128, 128), 0) + at
        for r in range(4):
            cols = slice(r * 128, r * 128 + 128)
            logit = tT[r, pl.ds(pl.multiple_of(shift + at, 8), 128), :]
            grad = sT[pl.ds(at, 128), cols] * sfac[:, cols] - jnp.exp(logit - tmax[:, cols]) * tfac[:, cols]
            grad = jnp.where(rows < ROWS, grad, 0.0)
            lhs[pl.ds(at, 128), cols] = grad.astype(BF16)
            dl[cols, pl.ds(at, 128)] = grad.T.astype(BF16)
        return 0

    lax.fori_loop(0, 8, dstep, 0)

    def ghpart(k, n):
        return jnp.dot(dl[:, 0:ROWS], w[:, pl.ds(pl.multiple_of(k * C + n * 256, 128), 256)],
                       preferred_element_type=F32)

    gc = []
    for p in range(3):
        for n in range(3):
            cs[p, :, n * 256:n * 256 + 256] = ghpart((1 - c) * 3 + p, n).astype(BF16)
        gc.append(send(cs.at[p], cr.at[p], sibling))
    g1 = {}
    for p in range(3):
        arrive([gc[p]])
        for n in range(3):
            cols = slice(n * 256, n * 256 + 256)
            total = ghpart(c * 3 + p, n) + cr[p, :, cols].astype(F32)
            s1[p, :, :, :, :, cols] = total.astype(BF16).reshape(4, 4, 2, 16, 256)
        if p == 0:
            g1[0] = [send(s1.at[0, d], r10.at[i], xp(d)) for i, d in enumerate(order)]
        elif p == 1:
            g1[1] = [send(s1.at[1, :, (y + d) % 4], r11.at[i], yp(d)) for i, d in enumerate(order)]
        else:
            g1[2] = []
            for i, d in enumerate(order):
                oz = (z + d) % 4
                ocols = pl.ds(pl.multiple_of((oz % 2) * HC, 128), HC)
                g1[2].append(send(s1.at[2, :, :, oz // 2, :, ocols], r12.at[i], zp(d)))

    out = [None, None]
    done = [0]

    def head(k):
        slot = done[0] % 2
        done[0] += 1
        if out[slot] is not None:
            out[slot].wait()

        def col(n, _):
            at = pl.ds(pl.multiple_of(n * 256, 256), 256)
            both = he[k, :, :, :, :, at].reshape(1024, 256)
            gb[slot, :, at] = jnp.dot(lhs[0:ROWS, :], both, preferred_element_type=F32).astype(BF16)
            return 0

        lax.fori_loop(0, 3, col, 0)
        out[slot] = local(gb.at[slot], head_out.at[:, pl.ds(pl.multiple_of(k * C, 128), C)])

    arrive(ex)
    ec = [send(he.at[c * 3 + p, pl.ds(5, 3)], he.at[c * 3 + p, pl.ds(5, 3)], sibling) for p in range(3)]
    head(c * 3)
    head(c * 3 + 1)

    def total(own, rec):
        return own.astype(F32) + sum(rec[i].astype(F32) for i in range(3))

    g2 = {}
    arrive(g1[0])
    s20[...] = total(s1[0, 0], r10).astype(BF16)
    g2[0] = [send(s20.at[(y + d) % 4], r20.at[i], yp(d)) for i, d in enumerate(order)]
    arrive(g1[1])
    s21[...] = total(s1[1, :, y], r11).astype(BF16)
    g2[1] = []
    for i, d in enumerate(order):
        oz = (z + d) % 4
        ocols = pl.ds(pl.multiple_of((oz % 2) * HC, 128), HC)
        g2[1].append(send(s21.at[:, oz // 2, :, ocols], r21.at[i], zp(d)))
    arrive(g1[2])
    s22[...] = total(s1[2, :, :, zh, :, zcols], r12).astype(BF16)
    g2[2] = [send(s22.at[d], r22.at[i], xp(d)) for i, d in enumerate(order)]

    head(c * 3 + 2)
    g3 = {}
    arrive(g2[0])
    s30[...] = total(s20[y], r20)
    g3[0] = []
    for i, d in enumerate(order):
        oz = (z + d) % 4
        ocols = pl.ds(pl.multiple_of((oz % 2) * HC, 128), HC)
        g3[0].append(send(s30.at[oz // 2, :, ocols], r3.at[0, i], zp(d)))
    arrive(g2[1])
    s31[...] = total(s21[:, zh, :, zcols], r21)
    g3[1] = [send(s31.at[d], r3.at[1, i], xp(d)) for i, d in enumerate(order)]
    arrive(g2[2])
    s32[...] = total(s22[0], r22)
    g3[2] = [send(s32.at[(y + d) % 4], r3.at[2, i], yp(d)) for i, d in enumerate(order)]

    arrive([ec[0]])
    head((1 - c) * 3)
    arrive(g3[0])
    go[k0, y, zh, :, zcols] = total(s30[zh, :, zcols], r3[0]).astype(BF16)
    part = go.at[k0, y, zh, :, zcols]
    a0 = [send(part, part, zp(d)) for d in order]
    arrive(g3[1])
    go[k1, y, zh, :, zcols] = total(s31[0], r3[1]).astype(BF16)
    part = go.at[k1, y, zh, :, zcols]
    a1 = [send(part, part, yp(d)) for d in order]
    arrive(g3[2])
    go[k2, y, zh, :, zcols] = total(s32[y], r3[2]).astype(BF16)
    part = go.at[k2, y, zh, :, zcols]
    a2 = [send(part, part, zp(d)) for d in order]
    arrive(a0)
    part = go.at[k0, y]
    b0 = [send(part, part, yp(d)) for d in order]
    arrive(a1)
    part = go.at[k1, :, zh, :, zcols]
    b1 = [send(part, part, zp(d)) for d in order]
    arrive(a2)
    part = go.at[k2, y]
    b2 = [send(part, part, yp(d)) for d in order]
    arrive([ec[1]])
    head((1 - c) * 3 + 1)
    arrive([ec[2]])
    head((1 - c) * 3 + 2)
    last = []
    b = {0: b0, 1: b1, 2: b2}
    for p in range(3):
        arrive(b[p])
        last.append(send(go.at[c * 3 + p], go.at[c * 3 + p], sibling))
    ends = []
    for p in range(3):
        at = pl.ds(pl.multiple_of((c * 3 + p) * C, 128), C)
        ends.append(local(go.at[c * 3 + p], gh_out.at[:, :, :, at]))
    for p in range(3):
        arrive([last[p]])
        at = pl.ds(pl.multiple_of(((1 - c) * 3 + p) * C, 128), C)
        ends.append(local(go.at[(1 - c) * 3 + p], gh_out.at[:, :, :, at]))
    for copy in ends + out:
        copy.wait()
    for copy in sent:
        copy.wait_send()


def shards(hidden, head_weight, teacher_logits, token_weight, token_ids, embed_grad):
    anywhere = pl.BlockSpec(memory_space=pl.ANY)
    inside = pl.BlockSpec(memory_space=pltpu.VMEM)
    V = pltpu.VMEM
    gh, head = pl.pallas_call(
        kernel,
        out_shape=(jax.ShapeDtypeStruct((4, 2, 16, D), BF16), jax.ShapeDtypeStruct((ROWS, D), BF16)),
        in_specs=[anywhere, anywhere, anywhere, inside, inside, anywhere],
        out_specs=(anywhere, anywhere),
        scratch_shapes=[
            V((6, 8, 4, 2, 16, C), BF16),
            V((ROWS, D), BF16),
            V((16, COLS), BF16),
            V((32, 16, WIDE), BF16),
            V((4, WIDE + 32, 128), F32),
            V((1024, 512), F32),
            V((1024, 1024), BF16),
            V((512, 1024), BF16),
            V((5, 8, 128), F32),
            V((5, 8, 128), F32),
            V((13, 8, 128), F32),
            V((13, 8, 128), F32),
            V((3, 512, C), BF16),
            V((3, 512, C), BF16),
            V((3, 4, 4, 2, 16, C), BF16),
            V((3, 4, 2, 16, C), BF16),
            V((3, 4, 2, 16, C), BF16),
            V((3, 4, 4, 16, HC), BF16),
            V((4, 2, 16, C), BF16),
            V((4, 2, 16, C), BF16),
            V((4, 4, 16, HC), BF16),
            V((3, 2, 16, C), BF16),
            V((3, 4, 16, HC), BF16),
            V((3, 4, 16, HC), BF16),
            V((2, 16, C), F32),
            V((4, 16, HC), F32),
            V((4, 16, HC), F32),
            V((3, 3, 16, HC), F32),
            V((6, 4, 2, 16, C), BF16),
            V((2, ROWS, C), BF16),
            pltpu.SemaphoreType.DMA((160,)),
            pltpu.SemaphoreType.DMA((160,)),
            pltpu.SemaphoreType.DMA((40,)),
        ],
        compiler_params=pltpu.CompilerParams(
            collective_id=0, has_side_effects=True, vmem_limit_bytes=60 * 2**20),
        cost_estimate=pl.CostEstimate(flops=19 * 10**9, bytes_accessed=30 * 10**6, transcendentals=2 * 10**6),
        name="distill",
    )(hidden.reshape(4, 2, 16, D), head_weight, teacher_logits, token_weight.reshape(4, 128),
      token_ids.astype(jnp.int32).reshape(4, 128), embed_grad.reshape(4, 2, 16, D))
    return gh.reshape(128, D), head


def solution(mesh):
    return jax.shard_map(
        shards,
        mesh=mesh,
        in_specs=(
            P("tok", None),
            P(("tok", "voc", "section"), None),
            P(("voc", "section"), "tok"),
            P(),
            P(),
            P("tok", None),
        ),
        out_specs=(P("tok", None), P(("tok", "voc", "section"), None)),
        check_vma=False,
    )
```

```python
import functools

import jax
import jax.numpy as jnp
from jax import lax
from jax.experimental import pallas as pl
from jax.experimental.pallas import tpu as pltpu
from jax.sharding import PartitionSpec as P

MESH = pl.DeviceIdType.MESH
D = 4608
ROWS = 1000
WIDE = 1152
COLS = 32000
C = 768
HC = 384
H1, H2, H3 = 3, 9, 15
LOW = -1e30
F32 = jnp.float32
BF16 = jnp.bfloat16


def merge(tiles):
    top = functools.reduce(jnp.maximum, [t[0:4] for t in tiles])
    total = sum(t[4:8] * jnp.exp(t[0:4] - top) for t in tiles)
    return top, total


def kernel(hidden, weight, teacher, tw, ids, embed, gh_out, head_out,
           he, w, tl, tr, tT, sT, lhs, dl, st, tt, sr, trr,
           cs, cr, s1, r10, r11, r12, s20, s21, s22, r20, r21, r22,
           r30, r31, r32, go, ssem, rsem, lsem):
    x = lax.axis_index("tok")
    v = lax.axis_index("voc")
    y = lax.axis_index("section")
    z, c = v // 2, v % 2
    j = v * 4 + y
    zh, zl = z // 2, z % 2
    zcols = pl.ds(pl.multiple_of(zl * HC, 128), HC)
    zlanes = pl.ds(pl.multiple_of(zl * 128, 128), 128)

    def xp(d):
        return ((x + d) % 4, v, y)

    def yp(d):
        return (x, v, (y + d) % 4)

    def zp(d):
        return (x, (v + 2 * d) % 8, y)

    def xcp(a, b):
        return ((x + a) % 4, z * 2 + (c + b) % 2, y)

    def yzp(a, b):
        return (x, (v + 2 * b) % 8, (y + a) % 4)

    def pp(d):
        other = (j + d) % 32
        return (x, other // 4, other % 4)

    sibling = (x, v + 1 - 2 * c, y)
    count = [0]
    sent = []

    def send(src, dst, to):
        i = count[0]
        count[0] += 1
        copy = pltpu.make_async_remote_copy(
            src, dst, ssem.at[i], rsem.at[i], device_id=to, device_id_type=MESH)
        copy.start()
        sent.append(copy)
        return copy

    lcount = [0]

    def local(src, dst):
        i = lcount[0]
        lcount[0] += 1
        copy = pltpu.make_async_copy(src, dst, lsem.at[i])
        copy.start()
        return copy

    def arrive(copies):
        for copy in copies:
            copy.wait_recv()

    own_hidden = [local(hidden.at[:, :, :, pl.ds(k * C, C)], he.at[k, 0]) for k in range(6)]
    own_teacher = local(teacher, tl)
    own_weight = local(weight, w)
    own_embed = [local(embed.at[:, :, :, pl.ds(k * C, C)], he.at[k, 4]) for k in range(6)]

    barrier = pltpu.get_barrier_semaphore()
    for d in range(1, 4):
        pl.semaphore_signal(barrier, inc=1, device_id=xp(d), device_id_type=MESH)
        pl.semaphore_signal(barrier, inc=1, device_id=xcp(d, 1), device_id_type=MESH)
    for d in range(1, 32):
        pl.semaphore_signal(barrier, inc=1, device_id=pp(d), device_id_type=MESH)
    pl.semaphore_wait(barrier, 37)

    for copy in own_hidden:
        copy.wait()
    k0, k1, k2 = c * 3, c * 3 + 1, c * 3 + 2
    order = (1, 3, 2)
    hx = {}
    for k, p in ((k1, 1), (k2, 2)):
        hx[p] = [send(he.at[k, 0, y, zh, :, zcols], he.at[k, 4 - d, y, zh, :, zcols], xp(d)) for d in order]

    own_teacher.wait()
    def max_step(i, acc):
        for q in range(10):
            acc = jnp.maximum(acc, tl[:, pl.ds(pl.multiple_of((i * 10 + q) * 128, 128), 128)].astype(F32))
        return acc

    ttop = jnp.max(lax.fori_loop(0, COLS // 1280, max_step, jnp.full((16, 128), LOW, F32)), axis=1, keepdims=True)

    def sum_step(i, acc):
        for q in range(10):
            acc = acc + jnp.exp(tl[:, pl.ds(pl.multiple_of((i * 10 + q) * 128, 128), 128)].astype(F32) - ttop)
        return acc

    ttot = jnp.sum(lax.fori_loop(0, COLS // 1280, sum_step, jnp.zeros((16, 128), F32)), axis=1, keepdims=True)
    lane = lax.broadcasted_iota(jnp.int32, (16, 128), 1)
    row = lax.broadcasted_iota(jnp.int32, (16, 128), 0)
    here = lane == row + (j % 8) * 16
    tt[0, 0:4] = jnp.full((4, 128), LOW, F32)
    tt[0, 4:8] = jnp.zeros((4, 128), F32)
    tt[0, pl.ds(j // 8, 1)] = jnp.max(jnp.where(here, jnp.broadcast_to(ttop, (16, 128)), LOW), axis=0, keepdims=True)
    tt[0, pl.ds(4 + j // 8, 1)] = jnp.sum(jnp.where(here, jnp.broadcast_to(ttot, (16, 128)), 0.0), axis=0, keepdims=True)

    def stage(buf, rec, n, base, peers):
        return [send(buf.at[n], rec.at[base + i], peer) for i, peer in enumerate(peers)]

    def join(buf, rec, n, base, copies):
        arrive(copies)
        top, total = merge([buf[n]] + [rec[base + i] for i in range(len(copies))])
        buf[n + 1, 0:4] = top
        buf[n + 1, 4:8] = total

    xcpeers = [xcp(a, b) for a in (1, 3, 2, 0) for b in range(2) if a or b]
    yzpeers = [yzp(a, b) for a in (2, 1, 3, 0) for b in (2, 1, 3, 0) if a or b]
    ts = stage(tt, trr, 0, 0, xcpeers)
    hx[0] = [send(he.at[k0, 0], he.at[k0, 4 - d], xp(d)) for d in order]

    def start_of(device):
        return pl.multiple_of(jnp.minimum(device * ROWS // 128 * 128, COLS - WIDE), 128)

    teach = []

    def send_teacher(ds):
        for d in ds:
            teach.append(send(tl.at[:, pl.ds(start_of((j + d) % 32), WIDE)], tr.at[j], pp(d)))

    own_block = local(tl.at[:, pl.ds(start_of(j), WIDE)], tr.at[j])
    arrive(hx[1])
    part = he.at[k1, pl.ds(1, 3), y, zh, :, zcols]
    hy1 = [send(part, part, yp(d)) for d in order]
    arrive(hx[2])
    part = he.at[k2, pl.ds(1, 3), y, zh, :, zcols]
    hz2 = [send(part, part, zp(d)) for d in order]
    join(tt, trr, 0, 0, ts)
    ts = stage(tt, trr, 1, 7, yzpeers)
    arrive(hy1)
    part = he.at[k1, pl.ds(1, 3), :, zh, :, zcols]
    hz1 = [send(part, part, zp(d)) for d in order]
    arrive(hz2)
    part = he.at[k2, pl.ds(1, 3), y]
    hy2 = [send(part, part, yp(d)) for d in order]


    def student(k, first):
        for half in range(2):
            tok = he[k, 2 * half:2 * half + 2].reshape(256, C)
            cols = slice(half * 256, half * 256 + 256)
            part = lax.dot_general(w[:, pl.ds(pl.multiple_of(k * C, 128), C)], tok,
                                   (((1,), (1,)), ((), ())), preferred_element_type=F32)
            if first:
                sT[0:ROWS, cols] = part
            else:
                sT[0:ROWS, cols] += part

    arrive(hx[0])
    hc = [send(he.at[k0, pl.ds(1, 3)], he.at[k0, pl.ds(1, 3)], sibling)]
    for copy in own_embed:
        copy.wait()
    ex, ef = {}, {}


    def embed_near(p):
        k = c * 3 + p
        ex[p] = [send(he.at[k, 4], he.at[k, 8 - d], xp(d)) for d in (1, 3)]

    def embed_far(p):
        k = c * 3 + p
        arrive(ex[p])
        low, high = pl.ds(0, HC), pl.ds(HC, HC)
        ef[p] = [send(he.at[k, 5, :, :, :, low], he.at[k, 6, :, :, :, low], xp(3)),
                 send(he.at[k, 7, :, :, :, high], he.at[k, 6, :, :, :, high], xp(1))]

    embed_near(0)
    embed_near(1)
    own_weight.wait()
    student(k0, True)
    arrive(hz1)
    hc.append(send(he.at[k1, pl.ds(1, 3)], he.at[k1, pl.ds(1, 3)], sibling))
    arrive(hy2)
    hc.append(send(he.at[k2, pl.ds(1, 3)], he.at[k2, pl.ds(1, 3)], sibling))
    send_teacher(range(1, 32))
    arrive([hc[0]])
    student((1 - c) * 3, False)
    student(k1, False)
    student(k2, False)
    for p in range(1, 3):
        arrive([hc[p]])
        student((1 - c) * 3 + p, False)

    def smax_step(i, acc):
        block = sT[pl.ds(pl.multiple_of(i * 40, 8), 40), :]
        for q in range(5):
            acc = jnp.maximum(acc, block[q * 8:q * 8 + 8])
        return acc

    stop_ = jnp.max(lax.fori_loop(0, 25, smax_step, jnp.full((8, 512), -3e38, F32)), axis=0, keepdims=True)

    def ssum_step(i, acc):
        at = pl.ds(pl.multiple_of(i * 40, 8), 40)
        block = jnp.exp(sT[at, :] - stop_)
        sT[at, :] = block
        for q in range(5):
            acc = acc + block[q * 8:q * 8 + 8]
        return acc

    stot = jnp.sum(lax.fori_loop(0, 25, ssum_step, jnp.zeros((8, 512), F32)), axis=0, keepdims=True)
    blocks = [(x + r) % 4 for r in range(4)]
    for r in range(4):
        st[0, pl.ds(blocks[r], 1)] = stop_[:, r * 128:r * 128 + 128]
        st[0, pl.ds(4 + blocks[r], 1)] = stot[:, r * 128:r * 128 + 128]
    ss = stage(st, sr, 0, 0, xcpeers)

    lhs[ROWS - 8:1024, :] = jnp.zeros((1024 - ROWS + 8, 1024), BF16)
    idrow = jnp.concatenate([ids[pl.ds(blocks[r], 1), :] for r in range(4)], axis=1) - (x * COLS + j * ROWS)

    def onehot(i, _):
        at = pl.multiple_of(i * 32, 32)
        rows = lax.broadcasted_iota(jnp.int32, (32, 512), 0) + at
        lhs[pl.ds(at, 32), 512:1024] = jnp.where((rows == idrow) & (rows < ROWS), 1.0, 0.0).astype(BF16)
        return 0

    lax.fori_loop(0, 32, onehot, 0)
    join(st, sr, 0, 0, ss)
    ss = stage(st, sr, 1, 7, yzpeers)
    embed_far(0)
    embed_near(2)

    own_block.wait()
    arrive(teach)
    tT[:, WIDE:WIDE + 32, :] = jnp.zeros((4, 32, 128), F32)
    for r in range(4):
        at = pl.multiple_of(blocks[r] * 8, 8)
        for q in range(9):
            tile = tr[pl.ds(at, 8), :, q * 128:q * 128 + 128].reshape(128, 128).astype(F32)
            tT[r, q * 128:q * 128 + 128, :] = tile.T

    join(tt, trr, 1, 7, ts)
    join(st, sr, 1, 7, ss)

    weights = tw[...]
    st[3, 0:4] = weights / st[2, 4:8]
    tt[3, 0:4] = weights / tt[2, 4:8]

    def token_row(ref, n, base):
        return jnp.concatenate([ref[n, pl.ds(base + blocks[r], 1), :] for r in range(4)], axis=1)

    sfac = jnp.exp(stop_ - token_row(st, 2, 0)) * token_row(st, 3, 0)
    tfac = token_row(tt, 3, 0)
    tmax = token_row(tt, 2, 0)

    shift = j * ROWS - start_of(j)

    def dstep(i, _):
        at = pl.multiple_of(i * 128, 128)
        rows = lax.broadcasted_iota(jnp.int32, (128, 128), 0) + at
        for r in range(4):
            cols = slice(r * 128, r * 128 + 128)
            logit = tT[r, pl.ds(pl.multiple_of(shift + at, 8), 128), :]
            grad = sT[pl.ds(at, 128), cols] * sfac[:, cols] - jnp.exp(logit - tmax[:, cols]) * tfac[:, cols]
            grad = jnp.where(rows < ROWS, grad, 0.0)
            lhs[pl.ds(at, 128), cols] = grad.astype(BF16)
            dl[cols, pl.ds(at, 128)] = grad.T.astype(BF16)
        return 0

    lax.fori_loop(0, 8, dstep, 0)

    def ghpart(k, n):
        return jnp.dot(dl[:, 0:ROWS], w[:, pl.ds(pl.multiple_of(k * C + n * 256, 128), 256)],
                       preferred_element_type=F32)

    def zpart(d):
        oz = (z + d) % 4
        return oz // 2, pl.ds(pl.multiple_of((oz % 2) * 128, 128), 128)

    g1 = {0: [], 1: [], 2: []}
    gc = {}

    def theirs(n):
        for p in range(3):
            cs[p, n] = ghpart((1 - c) * 3 + p, n).astype(BF16)
        gc[n] = [send(cs.at[p, n], cr.at[p, n], sibling) for p in range(3)]

    def ours(n):
        arrive(gc[n])
        for p in range(3):
            mine = ghpart(c * 3 + p, n) + cr[p, n].astype(F32)
            s1[p, n] = mine.astype(BF16).reshape(4, 4, 2, 16, 256)
        for i, d in enumerate(order):
            g1[0].append(send(s1.at[0, n, d], r10.at[i, n], xp(d)))
            g1[1].append(send(s1.at[1, n, :, (y + d) % 4], r11.at[i, n], yp(d)))
            oh, ol = zpart(d)
            g1[2].append(send(s1.at[2, n, :, :, oh, :, ol], r12.at[i, n], zp(d)))

    theirs(0)
    theirs(1)
    ours(0)
    theirs(2)
    ours(1)
    ours(2)

    pieces = [(c * 3 + p, n) for p in range(3) for n in range(3)]
    pieces += [((1 - c) * 3 + p, n) for p in range(3) for n in range(3)]
    done = [0]

    def head(upto):
        for k, n in pieces[done[0]:upto]:
            both = he[k, :, :, :, :, n * 256:n * 256 + 256].reshape(1024, 256)
            head_out[:, pl.ds(pl.multiple_of(k * C + n * 256, 128), 256)] = jnp.dot(
                lhs[0:ROWS, :], both, preferred_element_type=F32).astype(BF16)
        done[0] = upto

    embed_far(1)
    embed_far(2)
    ec = []

    def embed_over(p):
        arrive(ef[p])
        ec.append(send(he.at[c * 3 + p, pl.ds(5, 3)], he.at[c * 3 + p, pl.ds(5, 3)], sibling))

    embed_over(0)
    head(H1)

    def total(own, rec):
        return (own.astype(F32) + sum(rec[i].astype(F32) for i in range(3))).astype(BF16)

    g2 = {}
    arrive(g1[0])
    s20[...] = total(s1[0, :, 0], r10)
    g2[0] = []
    for i, d in enumerate(order):
        oh, ol = zpart(d)
        g2[0].append(send(s20.at[:, :, oh, :, ol], r20.at[i], zp(d)))
    arrive(g1[1])
    s21[...] = total(s1[1, :, :, y], r11)
    g2[1] = [send(s21.at[:, d], r21.at[i], xp(d)) for i, d in enumerate(order)]
    arrive(g1[2])
    s22[...] = total(s1[2, :, :, :, zh, :, zlanes], r12)
    g2[2] = [send(s22.at[:, d], r22.at[i], xp(d)) for i, d in enumerate(order)]
    embed_over(1)
    embed_over(2)
    head(H2)
    arrive(ec)

    g3 = {}
    arrive(g2[0])
    r30[y] = total(s20[:, :, zh, :, zlanes], r20)
    g3[0] = [send(r30.at[y], r30.at[y], yp(d)) for d in order]
    arrive(g2[1])
    r31[z] = total(s21[:, 0], r21)
    g3[1] = [send(r31.at[z], r31.at[z], zp(d)) for d in order]
    arrive(g2[2])
    r32[y] = total(s22[:, 0], r22)
    g3[2] = [send(r32.at[y], r32.at[y], yp(d)) for d in order]
    head(H3)

    def all4(rec):
        return sum(rec[i].astype(F32) for i in range(4)).astype(BF16)

    g4 = {}
    arrive(g3[0])
    go[k0, :, :, zh, :, zlanes] = all4(r30)
    part = go.at[k0, :, :, zh, :, zlanes]
    g4[0] = [send(part, part, zp(d)) for d in order]
    arrive(g3[1])
    go[k1, :, y] = all4(r31)
    part = go.at[k1, :, y]
    g4[1] = [send(part, part, yp(d)) for d in order]
    arrive(g3[2])
    go[k2, :, :, zh, :, zlanes] = all4(r32)
    part = go.at[k2, :, :, zh, :, zlanes]
    g4[2] = [send(part, part, zp(d)) for d in order]
    head(18)
    last = []
    for p in range(3):
        arrive(g4[p])
        last.append(send(go.at[c * 3 + p], go.at[c * 3 + p], sibling))

    def finish(k):
        for n in range(3):
            gh_out[:, :, :, pl.ds(pl.multiple_of(k * C + n * 256, 128), 256)] = go[k, n]

    for p in range(3):
        finish(c * 3 + p)
    for p in range(3):
        arrive([last[p]])
        finish((1 - c) * 3 + p)
    for copy in sent:
        copy.wait_send()


def shards(hidden, head_weight, teacher_logits, token_weight, token_ids, embed_grad):
    anywhere = pl.BlockSpec(memory_space=pl.ANY)
    inside = pl.BlockSpec(memory_space=pltpu.VMEM)
    V = pltpu.VMEM
    gh, head = pl.pallas_call(
        kernel,
        out_shape=(V((4, 2, 16, D), BF16), V((ROWS, D), BF16)),
        in_specs=[anywhere, anywhere, anywhere, inside, inside, anywhere],
        out_specs=(inside, inside),
        scratch_shapes=[
            V((6, 8, 4, 2, 16, C), BF16),
            V((ROWS, D), BF16),
            V((16, COLS), BF16),
            V((32, 16, WIDE), BF16),
            V((4, WIDE + 32, 128), F32),
            V((1024, 512), F32),
            V((1024, 1024), BF16),
            V((512, 1024), BF16),
            V((4, 8, 128), F32),
            V((4, 8, 128), F32),
            V((22, 8, 128), F32),
            V((22, 8, 128), F32),
            V((3, 3, 512, 256), BF16),
            V((3, 3, 512, 256), BF16),
            V((3, 3, 4, 4, 2, 16, 256), BF16),
            V((3, 3, 4, 2, 16, 256), BF16),
            V((3, 3, 4, 2, 16, 256), BF16),
            V((3, 3, 4, 4, 16, 128), BF16),
            V((3, 4, 2, 16, 256), BF16),
            V((3, 4, 2, 16, 256), BF16),
            V((3, 4, 4, 16, 128), BF16),
            V((3, 3, 4, 16, 128), BF16),
            V((3, 3, 2, 16, 256), BF16),
            V((3, 3, 4, 16, 128), BF16),
            V((4, 3, 4, 16, 128), BF16),
            V((4, 3, 2, 16, 256), BF16),
            V((4, 3, 4, 16, 128), BF16),
            V((6, 3, 4, 2, 16, 256), BF16),
            pltpu.SemaphoreType.DMA((220,)),
            pltpu.SemaphoreType.DMA((220,)),
            pltpu.SemaphoreType.DMA((40,)),
        ],
        compiler_params=pltpu.CompilerParams(
            collective_id=0, has_side_effects=True, vmem_limit_bytes=48 * 2**20),
        cost_estimate=pl.CostEstimate(flops=19 * 10**9, bytes_accessed=30 * 10**6, transcendentals=2 * 10**6),
        name="distill",
    )(hidden.reshape(4, 2, 16, D), head_weight, teacher_logits, token_weight.reshape(4, 128),
      token_ids.astype(jnp.int32).reshape(4, 128), embed_grad.reshape(4, 2, 16, D))
    return gh.reshape(128, D), head


def solution(mesh):
    return jax.shard_map(
        shards,
        mesh=mesh,
        in_specs=(
            P("tok", None),
            P(("tok", "voc", "section"), None),
            P(("voc", "section"), "tok"),
            P(),
            P(),
            P("tok", None),
        ),
        out_specs=(P("tok", None), P(("tok", "voc", "section"), None)),
        check_vma=False,
    )
```

```python
import functools

import jax
import jax.numpy as jnp
from jax import lax
from jax.experimental import pallas as pl
from jax.experimental.pallas import tpu as pltpu
from jax.sharding import PartitionSpec as P

MESH = pl.DeviceIdType.MESH
D = 4608
ROWS = 1000
WIDE = 1152
COLS = 32000
C = 768
HC = 384
EARLY = 3
H1, H2, H3 = 3, 9, 15
LOW = -1e30
F32 = jnp.float32
BF16 = jnp.bfloat16


def merge(tiles):
    top = functools.reduce(jnp.maximum, [t[0:4] for t in tiles])
    total = sum(t[4:8] * jnp.exp(t[0:4] - top) for t in tiles)
    return top, total


def kernel(hidden, weight, teacher, tw, ids, embed, gh_out, head_out,
           he, w, tl, tr, tT, sT, lhs, dl, st, tt, sr, trr,
           cs, cr, mine, s1, r10, r11, r12, s20, s21, s22, r20, r21, r22,
           r30, r31, r32, go, ssem, rsem, lsem):
    x = lax.axis_index("tok")
    v = lax.axis_index("voc")
    y = lax.axis_index("section")
    z, c = v // 2, v % 2
    j = v * 4 + y
    zh, zl = z // 2, z % 2
    zcols = pl.ds(pl.multiple_of(zl * HC, 128), HC)
    zlanes = pl.ds(pl.multiple_of(zl * 128, 128), 128)

    def xp(d):
        return ((x + d) % 4, v, y)

    def yp(d):
        return (x, v, (y + d) % 4)

    def zp(d):
        return (x, (v + 2 * d) % 8, y)

    def xcp(a, b):
        return ((x + a) % 4, z * 2 + (c + b) % 2, y)

    def yzp(a, b):
        return (x, (v + 2 * b) % 8, (y + a) % 4)

    def pp(d):
        other = (j + d) % 32
        return (x, other // 4, other % 4)

    sibling = (x, v + 1 - 2 * c, y)
    count = [0]
    sent = []

    def send(src, dst, to):
        i = count[0]
        count[0] += 1
        copy = pltpu.make_async_remote_copy(
            src, dst, ssem.at[i], rsem.at[i], device_id=to, device_id_type=MESH)
        copy.start()
        sent.append(copy)
        return copy

    lcount = [0]

    def local(src, dst):
        i = lcount[0]
        lcount[0] += 1
        copy = pltpu.make_async_copy(src, dst, lsem.at[i])
        copy.start()
        return copy

    def arrive(copies):
        for copy in copies:
            copy.wait_recv()

    own_hidden = [local(hidden.at[:, :, :, pl.ds(k * C, C)], he.at[k, 0]) for k in range(6)]
    own_teacher = local(teacher, tl)
    own_weight = local(weight, w)
    own_embed = [local(embed.at[:, :, :, pl.ds(k * C, C)], he.at[k, 4]) for k in range(6)]

    barrier = pltpu.get_barrier_semaphore()
    for d in range(1, 4):
        pl.semaphore_signal(barrier, inc=1, device_id=xp(d), device_id_type=MESH)
        pl.semaphore_signal(barrier, inc=1, device_id=xcp(d, 1), device_id_type=MESH)
    for d in range(1, 32):
        pl.semaphore_signal(barrier, inc=1, device_id=pp(d), device_id_type=MESH)
    pl.semaphore_wait(barrier, 37)

    for copy in own_hidden:
        copy.wait()
    k0, k1, k2 = c * 3, c * 3 + 1, c * 3 + 2
    order = (1, 3, 2)
    hx = {}
    for k, p in ((k1, 1), (k2, 2)):
        hx[p] = [send(he.at[k, 0, y, zh, :, zcols], he.at[k, 4 - d, y, zh, :, zcols], xp(d)) for d in order]

    own_teacher.wait()
    def max_step(i, acc):
        for q in range(10):
            acc = jnp.maximum(acc, tl[:, pl.ds(pl.multiple_of((i * 10 + q) * 128, 128), 128)].astype(F32))
        return acc

    ttop = jnp.max(lax.fori_loop(0, COLS // 1280, max_step, jnp.full((16, 128), LOW, F32)), axis=1, keepdims=True)

    def sum_step(i, acc):
        for q in range(10):
            acc = acc + jnp.exp(tl[:, pl.ds(pl.multiple_of((i * 10 + q) * 128, 128), 128)].astype(F32) - ttop)
        return acc

    ttot = jnp.sum(lax.fori_loop(0, COLS // 1280, sum_step, jnp.zeros((16, 128), F32)), axis=1, keepdims=True)
    lane = lax.broadcasted_iota(jnp.int32, (16, 128), 1)
    row = lax.broadcasted_iota(jnp.int32, (16, 128), 0)
    here = lane == row + (j % 8) * 16
    tt[0, 0:4] = jnp.full((4, 128), LOW, F32)
    tt[0, 4:8] = jnp.zeros((4, 128), F32)
    tt[0, pl.ds(j // 8, 1)] = jnp.max(jnp.where(here, jnp.broadcast_to(ttop, (16, 128)), LOW), axis=0, keepdims=True)
    tt[0, pl.ds(4 + j // 8, 1)] = jnp.sum(jnp.where(here, jnp.broadcast_to(ttot, (16, 128)), 0.0), axis=0, keepdims=True)

    def stage(buf, rec, n, base, peers):
        return [send(buf.at[n], rec.at[base + i], peer) for i, peer in enumerate(peers)]

    def join(buf, rec, n, base, copies):
        arrive(copies)
        top, total = merge([buf[n]] + [rec[base + i] for i in range(len(copies))])
        buf[n + 1, 0:4] = top
        buf[n + 1, 4:8] = total

    xcpeers = [xcp(a, b) for a in (1, 3, 2, 0) for b in range(2) if a or b]
    yzpeers = [yzp(a, b) for a in (2, 1, 3, 0) for b in (2, 1, 3, 0) if a or b]
    ts = stage(tt, trr, 0, 0, xcpeers)
    hx[0] = [send(he.at[k0, 0], he.at[k0, 4 - d], xp(d)) for d in order]

    def start_of(device):
        return pl.multiple_of(jnp.minimum(device * ROWS // 128 * 128, COLS - WIDE), 128)

    teach = []

    def send_teacher(ds):
        for d in ds:
            teach.append(send(tl.at[:, pl.ds(start_of((j + d) % 32), WIDE)], tr.at[j], pp(d)))

    send_teacher(range(1, 1 + EARLY))
    own_block = local(tl.at[:, pl.ds(start_of(j), WIDE)], tr.at[j])
    arrive(hx[1])
    part = he.at[k1, pl.ds(1, 3), y, zh, :, zcols]
    hy1 = [send(part, part, yp(d)) for d in order]
    arrive(hx[2])
    part = he.at[k2, pl.ds(1, 3), y, zh, :, zcols]
    hz2 = [send(part, part, zp(d)) for d in order]
    join(tt, trr, 0, 0, ts)
    ts = stage(tt, trr, 1, 7, yzpeers)
    arrive(hy1)
    part = he.at[k1, pl.ds(1, 3), :, zh, :, zcols]
    hz1 = [send(part, part, zp(d)) for d in order]
    over = {0: [], 1: [send(part, part, sibling)], 2: []}
    arrive(hz2)
    part = he.at[k2, pl.ds(1, 3), y]
    hy2 = [send(part, part, yp(d)) for d in order]
    over[2].append(send(part, part, sibling))


    def student(k, first):
        for half in range(2):
            tok = he[k, 2 * half:2 * half + 2].reshape(256, C)
            cols = slice(half * 256, half * 256 + 256)
            part = lax.dot_general(w[:, pl.ds(pl.multiple_of(k * C, 128), C)], tok,
                                   (((1,), (1,)), ((), ())), preferred_element_type=F32)
            if first:
                sT[0:ROWS, cols] = part
            else:
                sT[0:ROWS, cols] += part

    for copy, d in zip(hx[0], order):
        arrive([copy])
        over[0].append(send(he.at[k0, 4 - d], he.at[k0, 4 - d], sibling))
    for copy in own_embed:
        copy.wait()
    ex, ef = {}, {}


    def embed_near(p):
        k = c * 3 + p
        ex[p] = [send(he.at[k, 4], he.at[k, 8 - d], xp(d)) for d in (1, 3)]

    def embed_far(p):
        k = c * 3 + p
        arrive(ex[p])
        low, high = pl.ds(0, HC), pl.ds(HC, HC)
        ef[p] = [send(he.at[k, 5, :, :, :, low], he.at[k, 6, :, :, :, low], xp(3)),
                 send(he.at[k, 7, :, :, :, high], he.at[k, 6, :, :, :, high], xp(1))]

    embed_near(0)
    embed_near(1)
    own_weight.wait()
    student(k0, True)
    for i, d in enumerate(order):
        arrive([hz1[i]])
        oz = (z - d + 4) % 4
        part = he.at[k1, pl.ds(1, 3), :, oz // 2, :, pl.ds(pl.multiple_of((oz % 2) * HC, 128), HC)]
        over[1].append(send(part, part, sibling))
        arrive([hy2[i]])
        part = he.at[k2, pl.ds(1, 3), (y - d + 4) % 4]
        over[2].append(send(part, part, sibling))
    send_teacher(range(1 + EARLY, 32))
    arrive(over[0])
    student((1 - c) * 3, False)
    student(k1, False)
    student(k2, False)
    for p in range(1, 3):
        arrive(over[p])
        student((1 - c) * 3 + p, False)

    def smax_step(i, acc):
        block = sT[pl.ds(pl.multiple_of(i * 40, 8), 40), :]
        for q in range(5):
            acc = jnp.maximum(acc, block[q * 8:q * 8 + 8])
        return acc

    stop_ = jnp.max(lax.fori_loop(0, 25, smax_step, jnp.full((8, 512), -3e38, F32)), axis=0, keepdims=True)

    def ssum_step(i, acc):
        at = pl.ds(pl.multiple_of(i * 40, 8), 40)
        block = jnp.exp(sT[at, :] - stop_)
        sT[at, :] = block
        for q in range(5):
            acc = acc + block[q * 8:q * 8 + 8]
        return acc

    stot = jnp.sum(lax.fori_loop(0, 25, ssum_step, jnp.zeros((8, 512), F32)), axis=0, keepdims=True)
    blocks = [(x + r) % 4 for r in range(4)]
    for r in range(4):
        st[0, pl.ds(blocks[r], 1)] = stop_[:, r * 128:r * 128 + 128]
        st[0, pl.ds(4 + blocks[r], 1)] = stot[:, r * 128:r * 128 + 128]
    ss = stage(st, sr, 0, 0, xcpeers)

    lhs[ROWS - 8:1024, :] = jnp.zeros((1024 - ROWS + 8, 1024), BF16)
    idrow = jnp.concatenate([ids[pl.ds(blocks[r], 1), :] for r in range(4)], axis=1) - (x * COLS + j * ROWS)

    def onehot(i, _):
        at = pl.multiple_of(i * 32, 32)
        rows = lax.broadcasted_iota(jnp.int32, (32, 512), 0) + at
        lhs[pl.ds(at, 32), 512:1024] = jnp.where((rows == idrow) & (rows < ROWS), 1.0, 0.0).astype(BF16)
        return 0

    lax.fori_loop(0, 32, onehot, 0)
    join(st, sr, 0, 0, ss)
    ss = stage(st, sr, 1, 7, yzpeers)
    embed_far(0)
    embed_near(2)
    embed_far(1)

    own_block.wait()
    arrive(teach)
    tT[:, WIDE:WIDE + 32, :] = jnp.zeros((4, 32, 128), F32)
    for r in range(4):
        at = pl.multiple_of(blocks[r] * 8, 8)
        for q in range(9):
            tile = tr[pl.ds(at, 8), :, q * 128:q * 128 + 128].reshape(128, 128).astype(F32)
            tT[r, q * 128:q * 128 + 128, :] = tile.T

    join(tt, trr, 1, 7, ts)
    join(st, sr, 1, 7, ss)

    weights = tw[...]
    st[3, 0:4] = weights / st[2, 4:8]
    tt[3, 0:4] = weights / tt[2, 4:8]

    def token_row(ref, n, base):
        return jnp.concatenate([ref[n, pl.ds(base + blocks[r], 1), :] for r in range(4)], axis=1)

    sfac = jnp.exp(stop_ - token_row(st, 2, 0)) * token_row(st, 3, 0)
    tfac = token_row(tt, 3, 0)
    tmax = token_row(tt, 2, 0)

    shift = j * ROWS - start_of(j)

    def dstep(i, _):
        at = pl.multiple_of(i * 128, 128)
        rows = lax.broadcasted_iota(jnp.int32, (128, 128), 0) + at
        for r in range(4):
            cols = slice(r * 128, r * 128 + 128)
            logit = tT[r, pl.ds(pl.multiple_of(shift + at, 8), 128), :]
            grad = sT[pl.ds(at, 128), cols] * sfac[:, cols] - jnp.exp(logit - tmax[:, cols]) * tfac[:, cols]
            grad = jnp.where(rows < ROWS, grad, 0.0)
            lhs[pl.ds(at, 128), cols] = grad.astype(BF16)
            dl[cols, pl.ds(at, 128)] = grad.T.astype(BF16)
        return 0

    lax.fori_loop(0, 8, dstep, 0)

    def ghpart(k, n):
        return jnp.dot(dl[:, 0:ROWS], w[:, pl.ds(pl.multiple_of(k * C + n * 256, 128), 256)],
                       preferred_element_type=F32)

    def zpart(d):
        oz = (z + d) % 4
        return oz // 2, pl.ds(pl.multiple_of((oz % 2) * 128, 128), 128)

    g1 = {0: [], 1: [], 2: []}
    for n in range(3):
        gc = []
        for p in range(3):
            cs[p, n] = ghpart((1 - c) * 3 + p, n).astype(BF16)
            gc.append(send(cs.at[p, n], cr.at[p, n], sibling))
        for p in range(3):
            mine[p] = ghpart(c * 3 + p, n)
        for p in range(3):
            arrive([gc[p]])
            both = mine[p] + cr[p, n].astype(F32)
            s1[p, n] = both.astype(BF16).reshape(4, 4, 2, 16, 256)
            for i, d in enumerate(order):
                if p == 0:
                    g1[0].append(send(s1.at[0, n, d], r10.at[i, n], xp(d)))
                elif p == 1:
                    g1[1].append(send(s1.at[1, n, :, (y + d) % 4], r11.at[i, n], yp(d)))
                else:
                    oh, ol = zpart(d)
                    g1[2].append(send(s1.at[2, n, :, :, oh, :, ol], r12.at[i, n], zp(d)))

    pieces = [(c * 3 + p, n) for p in range(3) for n in range(3)]
    pieces += [((1 - c) * 3 + p, n) for p in range(3) for n in range(3)]
    done = [0]

    def head(upto):
        for k, n in pieces[done[0]:upto]:
            both = he[k, :, :, :, :, n * 256:n * 256 + 256].reshape(1024, 256)
            head_out[:, pl.ds(pl.multiple_of(k * C + n * 256, 128), 256)] = jnp.dot(
                lhs[0:ROWS, :], both, preferred_element_type=F32).astype(BF16)
        done[0] = upto

    embed_far(2)
    ec = []

    def embed_over(p):
        arrive(ef[p])
        ec.append(send(he.at[c * 3 + p, pl.ds(5, 3)], he.at[c * 3 + p, pl.ds(5, 3)], sibling))

    embed_over(0)
    head(H1)

    def total(own, rec):
        return (own.astype(F32) + sum(rec[i].astype(F32) for i in range(3))).astype(BF16)

    g2 = {}
    arrive(g1[0])
    s20[...] = total(s1[0, :, 0], r10)
    g2[0] = []
    for i, d in enumerate(order):
        oh, ol = zpart(d)
        g2[0].append(send(s20.at[:, :, oh, :, ol], r20.at[i], zp(d)))
    arrive(g1[1])
    s21[...] = total(s1[1, :, :, y], r11)
    g2[1] = [send(s21.at[:, d], r21.at[i], xp(d)) for i, d in enumerate(order)]
    arrive(g1[2])
    s22[...] = total(s1[2, :, :, :, zh, :, zlanes], r12)
    g2[2] = [send(s22.at[:, d], r22.at[i], xp(d)) for i, d in enumerate(order)]
    embed_over(1)
    embed_over(2)
    head(H2)
    arrive(ec)

    g3 = {}
    arrive(g2[0])
    r30[y] = total(s20[:, :, zh, :, zlanes], r20)
    g3[0] = [send(r30.at[y], r30.at[y], yp(d)) for d in order]
    arrive(g2[1])
    r31[z] = total(s21[:, 0], r21)
    g3[1] = [send(r31.at[z], r31.at[z], zp(d)) for d in order]
    arrive(g2[2])
    r32[y] = total(s22[:, 0], r22)
    g3[2] = [send(r32.at[y], r32.at[y], yp(d)) for d in order]
    head(H3)

    def all4(rec):
        return sum(rec[i].astype(F32) for i in range(4)).astype(BF16)

    g4, last = {}, {}
    arrive(g3[0])
    go[k0, :, :, zh, :, zlanes] = all4(r30)
    part = go.at[k0, :, :, zh, :, zlanes]
    g4[0] = [send(part, part, zp(d)) for d in order]
    last[0] = [send(part, part, sibling)]
    arrive(g3[1])
    go[k1, :, y] = all4(r31)
    part = go.at[k1, :, y]
    g4[1] = [send(part, part, yp(d)) for d in order]
    last[1] = [send(part, part, sibling)]
    arrive(g3[2])
    go[k2, :, :, zh, :, zlanes] = all4(r32)
    part = go.at[k2, :, :, zh, :, zlanes]
    g4[2] = [send(part, part, zp(d)) for d in order]
    last[2] = [send(part, part, sibling)]
    head(18)
    for i, d in enumerate(order):
        oz = (z - d + 4) % 4
        olanes = pl.ds(pl.multiple_of((oz % 2) * 128, 128), 128)
        parts = [go.at[k0, :, :, oz // 2, :, olanes], go.at[k1, :, (y - d + 4) % 4],
                 go.at[k2, :, :, oz // 2, :, olanes]]
        for p in range(3):
            arrive([g4[p][i]])
            last[p].append(send(parts[p], parts[p], sibling))

    def finish(k):
        for n in range(3):
            gh_out[:, :, :, pl.ds(pl.multiple_of(k * C + n * 256, 128), 256)] = go[k, n]

    for p in range(3):
        finish(c * 3 + p)
    for p in range(3):
        arrive(last[p])
        finish((1 - c) * 3 + p)
    for copy in sent:
        copy.wait_send()


def store(gh, head, gh_out, head_out, sems):
    copies = [pltpu.make_async_copy(gh, gh_out, sems.at[9])]
    for i in range(9):
        at = pl.ds(i * 512, 512)
        copies.append(pltpu.make_async_copy(head.at[:, at], head_out.at[:, at], sems.at[i]))
    for copy in copies:
        copy.start()
    for copy in copies:
        copy.wait()


def shards(hidden, head_weight, teacher_logits, token_weight, token_ids, embed_grad):
    anywhere = pl.BlockSpec(memory_space=pl.ANY)
    inside = pl.BlockSpec(memory_space=pltpu.VMEM)
    V = pltpu.VMEM
    gh, head = pl.pallas_call(
        kernel,
        out_shape=(V((4, 2, 16, D), BF16), V((ROWS, D), BF16)),
        in_specs=[anywhere, anywhere, anywhere, inside, inside, anywhere],
        out_specs=(inside, inside),
        scratch_shapes=[
            V((6, 8, 4, 2, 16, C), BF16),
            V((ROWS, D), BF16),
            V((16, COLS), BF16),
            V((32, 16, WIDE), BF16),
            V((4, WIDE + 32, 128), F32),
            V((1024, 512), F32),
            V((1024, 1024), BF16),
            V((512, 1024), BF16),
            V((4, 8, 128), F32),
            V((4, 8, 128), F32),
            V((22, 8, 128), F32),
            V((22, 8, 128), F32),
            V((3, 3, 512, 256), BF16),
            V((3, 3, 512, 256), BF16),
            V((3, 512, 256), F32),
            V((3, 3, 4, 4, 2, 16, 256), BF16),
            V((3, 3, 4, 2, 16, 256), BF16),
            V((3, 3, 4, 2, 16, 256), BF16),
            V((3, 3, 4, 4, 16, 128), BF16),
            V((3, 4, 2, 16, 256), BF16),
            V((3, 4, 2, 16, 256), BF16),
            V((3, 4, 4, 16, 128), BF16),
            V((3, 3, 4, 16, 128), BF16),
            V((3, 3, 2, 16, 256), BF16),
            V((3, 3, 4, 16, 128), BF16),
            V((4, 3, 4, 16, 128), BF16),
            V((4, 3, 2, 16, 256), BF16),
            V((4, 3, 4, 16, 128), BF16),
            V((6, 3, 4, 2, 16, 256), BF16),
            pltpu.SemaphoreType.DMA((220,)),
            pltpu.SemaphoreType.DMA((220,)),
            pltpu.SemaphoreType.DMA((40,)),
        ],
        compiler_params=pltpu.CompilerParams(
            collective_id=0, has_side_effects=True, vmem_limit_bytes=48 * 2**20),
        cost_estimate=pl.CostEstimate(flops=19 * 10**9, bytes_accessed=30 * 10**6, transcendentals=2 * 10**6),
        name="distill",
    )(hidden.reshape(4, 2, 16, D), head_weight, teacher_logits, token_weight.reshape(4, 128),
      token_ids.astype(jnp.int32).reshape(4, 128), embed_grad.reshape(4, 2, 16, D))
    return pl.pallas_call(
        store,
        out_shape=(jax.ShapeDtypeStruct((128, D), BF16), jax.ShapeDtypeStruct((ROWS, D), BF16)),
        in_specs=[anywhere, anywhere],
        out_specs=(anywhere, anywhere),
        scratch_shapes=[pltpu.SemaphoreType.DMA((10,))],
        compiler_params=pltpu.CompilerParams(vmem_limit_bytes=4 * 2**20),
        cost_estimate=pl.CostEstimate(flops=0, bytes_accessed=10 * 2**20, transcendentals=0),
        name="store",
    )(gh.reshape(128, D), head)


def solution(mesh):
    return jax.shard_map(
        shards,
        mesh=mesh,
        in_specs=(
            P("tok", None),
            P(("tok", "voc", "section"), None),
            P(("voc", "section"), "tok"),
            P(),
            P(),
            P("tok", None),
        ),
        out_specs=(P("tok", None), P(("tok", "voc", "section"), None)),
        check_vma=False,
    )
```

```python
import functools

import jax
import jax.numpy as jnp
from jax import lax
from jax.experimental import pallas as pl
from jax.experimental.pallas import tpu as pltpu
from jax.sharding import PartitionSpec as P

MESH = pl.DeviceIdType.MESH
D = 4608
ROWS = 1000
WIDE = 1152
COLS = 32000
C = 768
HC = 384
EARLY = 3
H1, H2, H3 = 3, 9, 15
LOW = -1e30
F32 = jnp.float32
BF16 = jnp.bfloat16


def merge(tiles):
    top = functools.reduce(jnp.maximum, [t[0:4] for t in tiles])
    total = sum(t[4:8] * jnp.exp(t[0:4] - top) for t in tiles)
    return top, total


def kernel(hidden, weight, teacher, tw, ids, embed, gh_out, head_out,
           he, w, tl, tr, tT, sT, lhs, dl, st, tt, sr, trr,
           cs, cr, mine, s1, r10, r11, r12, s20, s21, s22, r20, r21, r22,
           r30, r31, r32, go, ssem, rsem, lsem):
    x = lax.axis_index("tok")
    v = lax.axis_index("voc")
    y = lax.axis_index("section")
    z, c = v // 2, v % 2
    j = v * 4 + y
    zh, zl = z // 2, z % 2
    zcols = pl.ds(pl.multiple_of(zl * HC, 128), HC)
    zlanes = pl.ds(pl.multiple_of(zl * 128, 128), 128)

    def xp(d):
        return ((x + d) % 4, v, y)

    def yp(d):
        return (x, v, (y + d) % 4)

    def zp(d):
        return (x, (v + 2 * d) % 8, y)

    def xcp(a, b):
        return ((x + a) % 4, z * 2 + (c + b) % 2, y)

    def yzp(a, b):
        return (x, (v + 2 * b) % 8, (y + a) % 4)

    def pp(d):
        other = (j + d) % 32
        return (x, other // 4, other % 4)

    sibling = (x, v + 1 - 2 * c, y)
    count = [0]
    sent = []

    def send(src, dst, to):
        i = count[0]
        count[0] += 1
        copy = pltpu.make_async_remote_copy(
            src, dst, ssem.at[i], rsem.at[i], device_id=to, device_id_type=MESH)
        copy.start()
        sent.append(copy)
        return copy

    lcount = [0]

    def local(src, dst):
        i = lcount[0]
        lcount[0] += 1
        copy = pltpu.make_async_copy(src, dst, lsem.at[i])
        copy.start()
        return copy

    def arrive(copies):
        for copy in copies:
            copy.wait_recv()

    own_hidden = [local(hidden.at[:, :, :, pl.ds(k * C, C)], he.at[k, 0]) for k in range(6)]
    own_teacher = local(teacher, tl)
    own_weight = local(weight, w)
    own_embed = [local(embed.at[:, :, :, pl.ds(k * C, C)], he.at[k, 4]) for k in range(6)]

    barrier = pltpu.get_barrier_semaphore()
    for d in range(1, 4):
        pl.semaphore_signal(barrier, inc=1, device_id=xp(d), device_id_type=MESH)
        pl.semaphore_signal(barrier, inc=1, device_id=xcp(d, 1), device_id_type=MESH)
    for d in range(1, 32):
        pl.semaphore_signal(barrier, inc=1, device_id=pp(d), device_id_type=MESH)
    pl.semaphore_wait(barrier, 37)

    for copy in own_hidden:
        copy.wait()
    k0, k1, k2 = c * 3, c * 3 + 1, c * 3 + 2
    order = (1, 3, 2)
    hx = {}
    for k, p in ((k1, 1), (k2, 2)):
        hx[p] = [send(he.at[k, 0, y, zh, :, zcols], he.at[k, 4 - d, y, zh, :, zcols], xp(d)) for d in order]

    own_teacher.wait()
    def max_step(i, acc):
        for q in range(10):
            acc = jnp.maximum(acc, tl[:, pl.ds(pl.multiple_of((i * 10 + q) * 128, 128), 128)].astype(F32))
        return acc

    ttop = jnp.max(lax.fori_loop(0, COLS // 1280, max_step, jnp.full((16, 128), LOW, F32)), axis=1, keepdims=True)

    def sum_step(i, acc):
        for q in range(10):
            acc = acc + jnp.exp(tl[:, pl.ds(pl.multiple_of((i * 10 + q) * 128, 128), 128)].astype(F32) - ttop)
        return acc

    ttot = jnp.sum(lax.fori_loop(0, COLS // 1280, sum_step, jnp.zeros((16, 128), F32)), axis=1, keepdims=True)
    lane = lax.broadcasted_iota(jnp.int32, (16, 128), 1)
    row = lax.broadcasted_iota(jnp.int32, (16, 128), 0)
    here = lane == row + (j % 8) * 16
    tt[0, 0:4] = jnp.full((4, 128), LOW, F32)
    tt[0, 4:8] = jnp.zeros((4, 128), F32)
    tt[0, pl.ds(j // 8, 1)] = jnp.max(jnp.where(here, jnp.broadcast_to(ttop, (16, 128)), LOW), axis=0, keepdims=True)
    tt[0, pl.ds(4 + j // 8, 1)] = jnp.sum(jnp.where(here, jnp.broadcast_to(ttot, (16, 128)), 0.0), axis=0, keepdims=True)

    def stage(buf, rec, n, base, peers):
        return [send(buf.at[n], rec.at[base + i], peer) for i, peer in enumerate(peers)]

    def join(buf, rec, n, base, copies):
        arrive(copies)
        top, total = merge([buf[n]] + [rec[base + i] for i in range(len(copies))])
        buf[n + 1, 0:4] = top
        buf[n + 1, 4:8] = total

    xcpeers = [xcp(a, b) for a in (1, 3, 2, 0) for b in range(2) if a or b]
    yzpeers = [yzp(a, b) for a in (2, 1, 3, 0) for b in (2, 1, 3, 0) if a or b]
    ts = stage(tt, trr, 0, 0, xcpeers)
    hx[0] = [send(he.at[k0, 0], he.at[k0, 4 - d], xp(d)) for d in order]

    def start_of(device):
        return pl.multiple_of(jnp.minimum(device * ROWS // 128 * 128, COLS - WIDE), 128)

    teach = []

    def send_teacher(ds):
        for d in ds:
            teach.append(send(tl.at[:, pl.ds(start_of((j + d) % 32), WIDE)], tr.at[j], pp(d)))

    send_teacher(range(1, 1 + EARLY))
    own_block = local(tl.at[:, pl.ds(start_of(j), WIDE)], tr.at[j])
    arrive(hx[1])
    part = he.at[k1, pl.ds(1, 3), y, zh, :, zcols]
    hy1 = [send(part, part, yp(d)) for d in order]
    arrive(hx[2])
    part = he.at[k2, pl.ds(1, 3), y, zh, :, zcols]
    hz2 = [send(part, part, zp(d)) for d in order]
    join(tt, trr, 0, 0, ts)
    ts = stage(tt, trr, 1, 7, yzpeers)
    arrive(hy1)
    part = he.at[k1, pl.ds(1, 3), :, zh, :, zcols]
    hz1 = [send(part, part, zp(d)) for d in order]
    over = {0: [], 1: [send(part, part, sibling)], 2: []}
    arrive(hz2)
    part = he.at[k2, pl.ds(1, 3), y]
    hy2 = [send(part, part, yp(d)) for d in order]
    over[2].append(send(part, part, sibling))


    def student(k, first):
        for half in range(2):
            tok = he[k, 2 * half:2 * half + 2].reshape(256, C)
            cols = slice(half * 256, half * 256 + 256)
            part = lax.dot_general(w[:, pl.ds(pl.multiple_of(k * C, 128), C)], tok,
                                   (((1,), (1,)), ((), ())), preferred_element_type=F32)
            if first:
                sT[0:ROWS, cols] = part
            else:
                sT[0:ROWS, cols] += part

    for copy, d in zip(hx[0], order):
        arrive([copy])
        over[0].append(send(he.at[k0, 4 - d], he.at[k0, 4 - d], sibling))
    for copy in own_embed:
        copy.wait()
    ex, ef = {}, {}


    def embed_near(p):
        k = c * 3 + p
        ex[p] = [send(he.at[k, 4], he.at[k, 8 - d], xp(d)) for d in (1, 3)]

    def embed_far(p):
        k = c * 3 + p
        arrive(ex[p])
        low, high = pl.ds(0, HC), pl.ds(HC, HC)
        ef[p] = [send(he.at[k, 5, :, :, :, low], he.at[k, 6, :, :, :, low], xp(3)),
                 send(he.at[k, 7, :, :, :, high], he.at[k, 6, :, :, :, high], xp(1))]

    own_weight.wait()
    student(k0, True)
    for i, d in enumerate(order):
        arrive([hz1[i]])
        oz = (z - d + 4) % 4
        part = he.at[k1, pl.ds(1, 3), :, oz // 2, :, pl.ds(pl.multiple_of((oz % 2) * HC, 128), HC)]
        over[1].append(send(part, part, sibling))
        arrive([hy2[i]])
        part = he.at[k2, pl.ds(1, 3), (y - d + 4) % 4]
        over[2].append(send(part, part, sibling))
    send_teacher(range(1 + EARLY, 32))
    embed_near(0)
    embed_near(1)
    arrive(over[0])
    student((1 - c) * 3, False)
    student(k1, False)
    student(k2, False)
    for p in range(1, 3):
        arrive(over[p])
        student((1 - c) * 3 + p, False)

    def smax_step(i, acc):
        block = sT[pl.ds(pl.multiple_of(i * 40, 8), 40), :]
        for q in range(5):
            acc = jnp.maximum(acc, block[q * 8:q * 8 + 8])
        return acc

    stop_ = jnp.max(lax.fori_loop(0, 25, smax_step, jnp.full((8, 512), -3e38, F32)), axis=0, keepdims=True)

    def ssum_step(i, acc):
        at = pl.ds(pl.multiple_of(i * 40, 8), 40)
        block = jnp.exp(sT[at, :] - stop_)
        sT[at, :] = block
        for q in range(5):
            acc = acc + block[q * 8:q * 8 + 8]
        return acc

    stot = jnp.sum(lax.fori_loop(0, 25, ssum_step, jnp.zeros((8, 512), F32)), axis=0, keepdims=True)
    blocks = [(x + r) % 4 for r in range(4)]
    for r in range(4):
        st[0, pl.ds(blocks[r], 1)] = stop_[:, r * 128:r * 128 + 128]
        st[0, pl.ds(4 + blocks[r], 1)] = stot[:, r * 128:r * 128 + 128]
    ss = stage(st, sr, 0, 0, xcpeers)

    lhs[ROWS - 8:1024, :] = jnp.zeros((1024 - ROWS + 8, 1024), BF16)
    idrow = jnp.concatenate([ids[pl.ds(blocks[r], 1), :] for r in range(4)], axis=1) - (x * COLS + j * ROWS)

    def onehot(i, _):
        at = pl.multiple_of(i * 32, 32)
        rows = lax.broadcasted_iota(jnp.int32, (32, 512), 0) + at
        lhs[pl.ds(at, 32), 512:1024] = jnp.where((rows == idrow) & (rows < ROWS), 1.0, 0.0).astype(BF16)
        return 0

    lax.fori_loop(0, 32, onehot, 0)
    join(st, sr, 0, 0, ss)
    ss = stage(st, sr, 1, 7, yzpeers)
    embed_far(0)
    embed_near(2)
    embed_far(1)

    own_block.wait()
    arrive(teach)
    tT[:, WIDE:WIDE + 32, :] = jnp.zeros((4, 32, 128), F32)
    for r in range(4):
        at = pl.multiple_of(blocks[r] * 8, 8)
        for q in range(9):
            tile = tr[pl.ds(at, 8), :, q * 128:q * 128 + 128].reshape(128, 128).astype(F32)
            tT[r, q * 128:q * 128 + 128, :] = tile.T

    join(tt, trr, 1, 7, ts)
    join(st, sr, 1, 7, ss)

    weights = tw[...]
    st[3, 0:4] = weights / st[2, 4:8]
    tt[3, 0:4] = weights / tt[2, 4:8]

    def token_row(ref, n, base):
        return jnp.concatenate([ref[n, pl.ds(base + blocks[r], 1), :] for r in range(4)], axis=1)

    sfac = jnp.exp(stop_ - token_row(st, 2, 0)) * token_row(st, 3, 0)
    tfac = token_row(tt, 3, 0)
    tmax = token_row(tt, 2, 0)

    shift = j * ROWS - start_of(j)

    def dstep(i, _):
        at = pl.multiple_of(i * 128, 128)
        rows = lax.broadcasted_iota(jnp.int32, (128, 128), 0) + at
        for r in range(4):
            cols = slice(r * 128, r * 128 + 128)
            logit = tT[r, pl.ds(pl.multiple_of(shift + at, 8), 128), :]
            grad = sT[pl.ds(at, 128), cols] * sfac[:, cols] - jnp.exp(logit - tmax[:, cols]) * tfac[:, cols]
            grad = jnp.where(rows < ROWS, grad, 0.0)
            lhs[pl.ds(at, 128), cols] = grad.astype(BF16)
            dl[cols, pl.ds(at, 128)] = grad.T.astype(BF16)
        return 0

    lax.fori_loop(0, 8, dstep, 0)

    def ghpart(k, n):
        return jnp.dot(dl[:, 0:ROWS], w[:, pl.ds(pl.multiple_of(k * C + n * 256, 128), 256)],
                       preferred_element_type=F32)

    def zpart(d):
        oz = (z + d) % 4
        return oz // 2, pl.ds(pl.multiple_of((oz % 2) * 128, 128), 128)

    g1 = {0: [], 1: [], 2: []}
    for n in range(3):
        gc = []
        for p in range(3):
            cs[p, n] = ghpart((1 - c) * 3 + p, n).astype(BF16)
            gc.append(send(cs.at[p, n], cr.at[p, n], sibling))
        for p in range(3):
            mine[p] = ghpart(c * 3 + p, n)
        for p in range(3):
            arrive([gc[p]])
            both = mine[p] + cr[p, n].astype(F32)
            s1[p, n] = both.astype(BF16).reshape(4, 4, 2, 16, 256)
            for i, d in enumerate(order):
                if p == 0:
                    g1[0].append(send(s1.at[0, n, d], r10.at[i, n], xp(d)))
                elif p == 1:
                    g1[1].append(send(s1.at[1, n, :, (y + d) % 4], r11.at[i, n], yp(d)))
                else:
                    oh, ol = zpart(d)
                    g1[2].append(send(s1.at[2, n, :, :, oh, :, ol], r12.at[i, n], zp(d)))

    pieces = [(c * 3 + p, n) for p in range(3) for n in range(3)]
    pieces += [((1 - c) * 3 + p, n) for p in range(3) for n in range(3)]
    done = [0]

    def head(upto):
        for k, n in pieces[done[0]:upto]:
            both = he[k, :, :, :, :, n * 256:n * 256 + 256].reshape(1024, 256)
            head_out[:, pl.ds(pl.multiple_of(k * C + n * 256, 128), 256)] = jnp.dot(
                lhs[0:ROWS, :], both, preferred_element_type=F32).astype(BF16)
        done[0] = upto

    embed_far(2)
    ec = []

    def embed_over(p):
        arrive(ef[p])
        ec.append(send(he.at[c * 3 + p, pl.ds(5, 3)], he.at[c * 3 + p, pl.ds(5, 3)], sibling))

    embed_over(0)
    head(H1)

    def total(own, rec):
        return (own.astype(F32) + sum(rec[i].astype(F32) for i in range(3))).astype(BF16)

    g2 = {}
    arrive(g1[0])
    s20[...] = total(s1[0, :, 0], r10)
    g2[0] = []
    for i, d in enumerate(order):
        oh, ol = zpart(d)
        g2[0].append(send(s20.at[:, :, oh, :, ol], r20.at[i], zp(d)))
    arrive(g1[1])
    s21[...] = total(s1[1, :, :, y], r11)
    g2[1] = [send(s21.at[:, d], r21.at[i], xp(d)) for i, d in enumerate(order)]
    arrive(g1[2])
    s22[...] = total(s1[2, :, :, :, zh, :, zlanes], r12)
    g2[2] = [send(s22.at[:, d], r22.at[i], xp(d)) for i, d in enumerate(order)]
    embed_over(1)
    embed_over(2)
    head(H2)
    arrive(ec)

    g3 = {}
    arrive(g2[0])
    r30[y] = total(s20[:, :, zh, :, zlanes], r20)
    g3[0] = [send(r30.at[y], r30.at[y], yp(d)) for d in order]
    arrive(g2[1])
    r31[z] = total(s21[:, 0], r21)
    g3[1] = [send(r31.at[z], r31.at[z], zp(d)) for d in order]
    arrive(g2[2])
    r32[y] = total(s22[:, 0], r22)
    g3[2] = [send(r32.at[y], r32.at[y], yp(d)) for d in order]
    head(H3)

    def all4(rec):
        return sum(rec[i].astype(F32) for i in range(4)).astype(BF16)

    g4, last = {}, {}
    arrive(g3[0])
    go[k0, :, :, zh, :, zlanes] = all4(r30)
    part = go.at[k0, :, :, zh, :, zlanes]
    g4[0] = [send(part, part, zp(d)) for d in order]
    last[0] = [send(part, part, sibling)]
    arrive(g3[1])
    go[k1, :, y] = all4(r31)
    part = go.at[k1, :, y]
    g4[1] = [send(part, part, yp(d)) for d in order]
    last[1] = [send(part, part, sibling)]
    arrive(g3[2])
    go[k2, :, :, zh, :, zlanes] = all4(r32)
    part = go.at[k2, :, :, zh, :, zlanes]
    g4[2] = [send(part, part, zp(d)) for d in order]
    last[2] = [send(part, part, sibling)]
    head(18)
    for i, d in enumerate(order):
        oz = (z - d + 4) % 4
        olanes = pl.ds(pl.multiple_of((oz % 2) * 128, 128), 128)
        parts = [go.at[k0, :, :, oz // 2, :, olanes], go.at[k1, :, (y - d + 4) % 4],
                 go.at[k2, :, :, oz // 2, :, olanes]]
        for p in range(3):
            arrive([g4[p][i]])
            last[p].append(send(parts[p], parts[p], sibling))

    def finish(k):
        for n in range(3):
            gh_out[:, :, :, pl.ds(pl.multiple_of(k * C + n * 256, 128), 256)] = go[k, n]

    for p in range(3):
        finish(c * 3 + p)
    for p in range(3):
        arrive(last[p])
        finish((1 - c) * 3 + p)
    for copy in sent:
        copy.wait_send()


def store(gh, head, gh_out, head_out, sems):
    copies = [pltpu.make_async_copy(gh, gh_out, sems.at[9])]
    for i in range(9):
        at = pl.ds(i * 512, 512)
        copies.append(pltpu.make_async_copy(head.at[:, at], head_out.at[:, at], sems.at[i]))
    for copy in copies:
        copy.start()
    for copy in copies:
        copy.wait()


def shards(hidden, head_weight, teacher_logits, token_weight, token_ids, embed_grad):
    anywhere = pl.BlockSpec(memory_space=pl.ANY)
    inside = pl.BlockSpec(memory_space=pltpu.VMEM)
    V = pltpu.VMEM
    gh, head = pl.pallas_call(
        kernel,
        out_shape=(V((4, 2, 16, D), BF16), V((ROWS, D), BF16)),
        in_specs=[anywhere, anywhere, anywhere, inside, inside, anywhere],
        out_specs=(inside, inside),
        scratch_shapes=[
            V((6, 8, 4, 2, 16, C), BF16),
            V((ROWS, D), BF16),
            V((16, COLS), BF16),
            V((32, 16, WIDE), BF16),
            V((4, WIDE + 32, 128), F32),
            V((1024, 512), F32),
            V((1024, 1024), BF16),
            V((512, 1024), BF16),
            V((4, 8, 128), F32),
            V((4, 8, 128), F32),
            V((22, 8, 128), F32),
            V((22, 8, 128), F32),
            V((3, 3, 512, 256), BF16),
            V((3, 3, 512, 256), BF16),
            V((3, 512, 256), F32),
            V((3, 3, 4, 4, 2, 16, 256), BF16),
            V((3, 3, 4, 2, 16, 256), BF16),
            V((3, 3, 4, 2, 16, 256), BF16),
            V((3, 3, 4, 4, 16, 128), BF16),
            V((3, 4, 2, 16, 256), BF16),
            V((3, 4, 2, 16, 256), BF16),
            V((3, 4, 4, 16, 128), BF16),
            V((3, 3, 4, 16, 128), BF16),
            V((3, 3, 2, 16, 256), BF16),
            V((3, 3, 4, 16, 128), BF16),
            V((4, 3, 4, 16, 128), BF16),
            V((4, 3, 2, 16, 256), BF16),
            V((4, 3, 4, 16, 128), BF16),
            V((6, 3, 4, 2, 16, 256), BF16),
            pltpu.SemaphoreType.DMA((220,)),
            pltpu.SemaphoreType.DMA((220,)),
            pltpu.SemaphoreType.DMA((40,)),
        ],
        compiler_params=pltpu.CompilerParams(
            collective_id=0, has_side_effects=True, vmem_limit_bytes=48 * 2**20),
        cost_estimate=pl.CostEstimate(flops=19 * 10**9, bytes_accessed=30 * 10**6, transcendentals=2 * 10**6),
        name="distill",
    )(hidden.reshape(4, 2, 16, D), head_weight, teacher_logits, token_weight.reshape(4, 128),
      token_ids.astype(jnp.int32).reshape(4, 128), embed_grad.reshape(4, 2, 16, D))
    return pl.pallas_call(
        store,
        out_shape=(jax.ShapeDtypeStruct((128, D), BF16), jax.ShapeDtypeStruct((ROWS, D), BF16)),
        in_specs=[anywhere, anywhere],
        out_specs=(anywhere, anywhere),
        scratch_shapes=[pltpu.SemaphoreType.DMA((10,))],
        compiler_params=pltpu.CompilerParams(vmem_limit_bytes=4 * 2**20),
        cost_estimate=pl.CostEstimate(flops=0, bytes_accessed=10 * 2**20, transcendentals=0),
        name="store",
    )(gh.reshape(128, D), head)


def solution(mesh):
    return jax.shard_map(
        shards,
        mesh=mesh,
        in_specs=(
            P("tok", None),
            P(("tok", "voc", "section"), None),
            P(("voc", "section"), "tok"),
            P(),
            P(),
            P("tok", None),
        ),
        out_specs=(P("tok", None), P(("tok", "voc", "section"), None)),
        check_vma=False,
    )
```
